256 devices in a mesh: section: 16 (over z_lo, x), dp: 16 (over z_hi, y, core).
Axes of the slice: x: 4, y: 4, z: 8 (z_hi: 2, z_lo: 4; z = z_hi * 4 + z_lo), core: 2. Of those that a mesh axis runs over, the one named last changes fastest.
Arguments:
- images: bfloat16 [4, 1024, 1664], P(None, 'dp'), may hold values from -6 to 6
- cotangent: bfloat16 [4, 1024, 1664], P(None, 'dp'), may hold values from -6 to 6
- weight: float32 [16, 2, 1664, 1664], P('section', None, 'dp'), may hold values from -5 to 5
- first_moment: float32 [16, 2, 1664, 1664], P('section', None, 'dp'), may hold values from -0.6 to 0.6
- second_moment: float32 [16, 2, 1664, 1664], P('section', None, 'dp'), may hold values from 0.005 to 0.1
- norm_gain: float32 [16, 2, 1664], P('section'), may hold values from 0.5 to 1.5
- layer_scale: float32 [16, 2, 1664], P('section'), may hold values from 0.1 to 0.5
- count_before: int32 [16], replicated, may hold values from 1 to 2, as said below
- count_after: int32 [16], replicated, may hold values from 1 to 2, as said below
- micro_order: int32 [4], replicated, may hold values from 0 to 3, each once
Outputs:
- new_weight: float32 [16, 2, 1664, 1664], P('section', None, 'dp')
- new_first_moment: float32 [16, 2, 1664, 1664], P('section', None, 'dp')
- new_second_moment: float32 [16, 2, 1664, 1664], P('section', None, 'dp')
The draws below stay inside these ranges and needn't reach their ends.
Inputs may be any that keep to these rules, and one draw needn't show every extreme that they name: Every section holds one or two layers in both tables and both totals are equal. For each section s the sum of count_before over sections 0 .. s equals that of count_after or exceeds it by one, and they are equal at the last section: a layer moves at most one section, to the next higher index. In every draw section 0 passes its last layer to section 1, section 14 passes its last layer to the last section, and some section holds two layers in each table. `count_after`: see count_before. `micro_order`: each micro-batch once.
All inputs are finite; a program needn't handle non-finite values.
Results may differ from the reference program's by a relative error of at most 0.022.
Values may be sent and summed in bfloat16 or wider, within the bound.
No kernel may reach another device: no remote copies, remote signals or barrier semaphores. Data moves between devices by JAX's collectives and lax.ppermute only.
A program may use at most 128 MiB of HBM per device.

```python
import math
import jax
import jax.numpy as jnp
from jax import lax

D = 1664
CAP = 2
MICRO = 4
ROWS = 64
TOK = 1024
N_SECTION = 16
N_DP = 16


def layer_tables(key):
    key_bits = jax.random.fold_in(key, 101)
    key_free = jax.random.fold_in(key, 202)
    section_ids = jnp.arange(N_SECTION, dtype=jnp.int32)
    shifted = jax.random.randint(key_bits, (N_SECTION,), 0, 2, dtype=jnp.int32)
    forced = (section_ids == 0) | (section_ids == N_SECTION - 2)
    shifted = jnp.where(forced, 1, shifted)
    shifted = jnp.where(section_ids == N_SECTION - 1, 0, shifted)
    previous = jnp.concatenate([jnp.zeros((1,), jnp.int32), shifted[:-1]])
    free_count = jax.random.randint(key_free, (N_SECTION,), 1, 3, dtype=jnp.int32)
    before_table = jnp.where((shifted == 1) & (previous == 0), 2, jnp.where((shifted == 0) & (previous == 1), 1, free_count))
    after_table = before_table - shifted + previous
    return (before_table.astype(jnp.int32), after_table.astype(jnp.int32))


def draw_count_before(key, part):
    tables = layer_tables(key)
    return tables[0]


def draw_count_after(key, part):
    tables = layer_tables(key)
    return tables[1]


def spiked(array, rng, source, target, blocks, factor):
    owner, partner = [(jnp.arange(array.shape[dim]) // (array.shape[dim] // blocks)).reshape([-1 if axis == dim else 1 for axis in range(array.ndim)]) for dim in (source, target)]
    chosen = jax.random.permutation(rng, blocks)[partner]
    strong = (owner == chosen) | (owner == (partner + blocks // 2) % blocks)
    return jnp.where(strong, factor * array, array)


def level_of(rng, shape, shards, least, high):
    level, own = 1.0, jax.random.fold_in(rng, 6)
    for axis_at, shards_of in shards:
        heights = jnp.exp(jax.random.uniform(jax.random.fold_in(own, axis_at), (shards_of,), jnp.float32, least / len(shards), high / len(shards)))
        level = level * jnp.repeat(heights, shape[axis_at] // shards_of).reshape([-1 if axis == axis_at else 1 for axis in range(len(shape))])
    return level


def centred(own_key, dims, width, most, pieces=(), held_as=jnp.bfloat16):
    values = width * jax.random.normal(own_key, dims, jnp.float32)
    if pieces:
        values = values * level_of(own_key, dims, pieces, -0.22, 0.18)
    return jnp.clip(values, -most, most).astype(held_as)


def gaussian_with(stream_key, shape, spread, reach, shards, heavy, held_as=jnp.bfloat16):
    array = spread * jax.random.normal(stream_key, shape, jnp.float32)
    if shards:
        array = array * level_of(stream_key, shape, shards, -0.22, 0.18)
    return jnp.clip(spiked(array, jax.random.fold_in(stream_key, 3), *heavy), -reach, reach).astype(held_as)


def setup_inputs(seed: int = 0) -> dict:
    arg_keys = jax.random.split(jax.random.key(seed), 11)
    images = gaussian_with(arg_keys[0], (MICRO, TOK, D), 1.0, 6.0, ((1, 16),), (1, 2, 16, 2.0))
    cotangent = centred(arg_keys[1], (MICRO, TOK, D), 1.0, 6.0, ((1, 16),))
    weight = centred(arg_keys[2], (N_SECTION, CAP, D, D), 1.0, 5.0, ((0, 16), (2, 16)), jnp.float32)
    first_moment = centred(arg_keys[3], (N_SECTION, CAP, D, D), 0.1, 0.6, ((0, 16), (2, 16)), jnp.float32)
    second_moment = jnp.clip(jnp.exp(math.log(0.1) - 2.9957323 * jax.random.uniform(arg_keys[4], (N_SECTION, CAP, D, D), jnp.float32) ** level_of(arg_keys[4], (N_SECTION, CAP, D, D), ((0, 16), (2, 16)), -0.2, 0.2)), 0.005, 0.1)
    norm_gain = jnp.clip(1.0 + 0.1 * jax.random.normal(arg_keys[5], (N_SECTION, CAP, D), jnp.float32), 0.5, 1.5)
    layer_scale = jnp.clip(0.1 + 0.4 * jax.random.uniform(arg_keys[6], (N_SECTION, CAP, D), jnp.float32) ** level_of(arg_keys[6], (N_SECTION, CAP, D), ((0, 16),), -0.2, 0.2), 0.1, 0.5)
    count_before = draw_count_before(jax.random.fold_in(arg_keys[10], 71), 0)
    count_after = draw_count_after(jax.random.fold_in(arg_keys[10], 71), 0)
    micro_order = jax.random.permutation(arg_keys[9], MICRO).astype(jnp.int32)
    return dict(images=images, cotangent=cotangent, weight=weight, first_moment=first_moment, second_moment=second_moment, norm_gain=norm_gain, layer_scale=layer_scale, count_before=count_before, count_after=count_after, micro_order=micro_order)


NORM_EPS = 1e-06
GELU_COEF = 0.7978845608028654
GELU_CUBE = 0.044715
FIRST_DECAY_RATE = 0.9
BETA_TWO = 0.95
LEARN_RATE = 0.1
ADAM_EPS = 1e-08
WEIGHT_DECAY = 0.05

def gelu_pair(hidden):
    tanh_val = jnp.tanh(GELU_COEF * (hidden + GELU_CUBE * hidden * hidden * hidden))
    activated = 0.5 * hidden * (1.0 + tanh_val)
    gradient_slope = 0.5 * (1.0 + tanh_val) + 0.5 * hidden * (1.0 - tanh_val * tanh_val) * GELU_COEF * (1.0 + 3.0 * GELU_CUBE * hidden * hidden)
    return (activated, gradient_slope)

def normalize(inputs, gain_row):
    widened = inputs.astype(jnp.float32)
    inv_rms = lax.rsqrt(lax.optimization_barrier(jnp.mean(widened * widened, axis=-1, keepdims=True)) + NORM_EPS)
    normed = widened * inv_rms
    return (widened, inv_rms, normed, (normed * gain_row).astype(jnp.bfloat16))

def layer_forward(inputs, weight_bf, gain_row, scale_row):
    widened, inv_rms, normed, scaled = normalize(inputs, gain_row)
    hidden = jnp.dot(scaled, weight_bf, preferred_element_type=jnp.float32) * weight_bf.shape[0] ** (-0.5)
    activated, gradient_slope = gelu_pair(hidden)
    return (widened + scale_row * activated).astype(jnp.bfloat16)

def layer_backward(inputs, upstream, weight_bf, gain_row, scale_row):
    widened, inv_rms, normed, scaled = normalize(inputs, gain_row)
    factor = weight_bf.shape[0] ** (-0.5)
    hidden = jnp.dot(scaled, weight_bf, preferred_element_type=jnp.float32) * factor
    activated, gradient_slope = gelu_pair(hidden)
    upstream_wide = upstream.astype(jnp.float32)
    signal = (upstream_wide * scale_row * gradient_slope * factor).astype(jnp.bfloat16)
    backward_term = lax.dot_general(signal, weight_bf, (((1,), (1,)), ((), ())), preferred_element_type=jnp.float32) * gain_row
    projection = lax.optimization_barrier(jnp.mean(backward_term * normed, axis=-1, keepdims=True))
    result = (upstream_wide + inv_rms * (backward_term - normed * projection)).astype(jnp.bfloat16)
    return (result, scaled, signal)

def reference(images, cotangent, weight, first_moment, second_moment, norm_gain, layer_scale, count_before, count_after, micro_order):
    slot_total = N_SECTION * CAP
    inputs = jnp.take(images, micro_order, axis=0).reshape(MICRO * TOK, D)
    weights_bf = weight.astype(jnp.bfloat16).reshape(slot_total, D, D)
    gains = norm_gain.reshape(slot_total, D)
    scales = layer_scale.reshape(slot_total, D)
    slot_ids = jnp.arange(CAP, dtype=jnp.int32)
    live_before = (slot_ids[None, :] < count_before[:, None]).reshape(slot_total)
    live_after = (slot_ids[None, :] < count_after[:, None]).reshape(slot_total)

    def forward_step(carried, packed):
        weight_bf, gain_row, scale_row, is_live = packed

        def active_layer(values):
            return layer_forward(values, weight_bf, gain_row, scale_row)

        def skip_layer(values):
            return values
        return (lax.cond(is_live, active_layer, skip_layer, carried), carried)
    encoded, stored = lax.scan(forward_step, inputs, (weights_bf, gains, scales, live_before))

    def backward_step(upstream, packed):
        layer_in, weight_bf, gain_row, scale_row, is_live = packed

        def active_layer(values):
            result, scaled, signal = layer_backward(layer_in, values, weight_bf, gain_row, scale_row)
            left = scaled.reshape(MICRO, N_DP, ROWS, D).astype(jnp.float32)
            right = signal.reshape(MICRO, N_DP, ROWS, D).astype(jnp.float32)
            partials = jnp.einsum('mrtd,mrte->rde', left, right)
            rounded = lax.optimization_barrier(partials.astype(jnp.bfloat16))
            return (result, lax.optimization_barrier(jnp.sum(rounded.astype(jnp.float32), axis=0)))

        def skip_layer(values):
            return (values, jnp.zeros((D, D), jnp.float32))
        return lax.cond(is_live, active_layer, skip_layer, upstream)
    unused, gradients = lax.scan(backward_step, cotangent.reshape(MICRO * TOK, D), (stored, weights_bf, gains, scales, live_before), reverse=True)
    weight_flat = weight.reshape(slot_total, D, D)
    first_flat = FIRST_DECAY_RATE * first_moment.reshape(slot_total, D, D) + (1.0 - FIRST_DECAY_RATE) * gradients
    second_flat = BETA_TWO * second_moment.reshape(slot_total, D, D) + (1.0 - BETA_TWO) * gradients * gradients
    updated_flat = weight_flat - LEARN_RATE * (first_flat / (jnp.sqrt(second_flat) + ADAM_EPS) + WEIGHT_DECAY * weight_flat)
    start_before = (jnp.cumsum(count_before) - count_before).astype(jnp.int32)
    start_after = (jnp.cumsum(count_after) - count_after).astype(jnp.int32)
    layer_before = (start_before[:, None] + slot_ids[None, :]).reshape(slot_total)
    layer_after = (start_after[:, None] + slot_ids[None, :]).reshape(slot_total)
    matching = live_after[:, None] & live_before[None, :] & (layer_after[:, None] == layer_before[None, :])
    flat_ids = jnp.arange(slot_total, dtype=jnp.int32)
    source = lax.optimization_barrier(jnp.sum(jnp.where(matching, flat_ids[None, :], 0), axis=1)).astype(jnp.int32)

    def to_after(values):
        picked = jnp.take(values, source, axis=0)
        return jnp.where(live_after[:, None, None], picked, 0.0).reshape(N_SECTION, CAP, D, D)
    return (to_after(updated_flat), to_after(first_flat), to_after(second_flat))
```

```python
import jax
import jax.numpy as jnp
from jax import lax
from jax.experimental import pallas as pl
from jax.experimental.pallas import tpu as pltpu
from jax.sharding import Mesh, PartitionSpec as P

NORM_EPS = 1e-06
GELU_COEF = 0.7978845608028654
GELU_CUBE = 0.044715
FIRST_DECAY_RATE = 0.9
BETA_TWO = 0.95
LEARN_RATE = 0.1
ADAM_EPS = 1e-08
WEIGHT_DECAY = 0.05

NZL, NX, NZH, NY, NC = 4, 4, 2, 4, 2
SLOTS = 2
LAYERS = NX * SLOTS
BF = jnp.bfloat16
F32 = jnp.float32
VMEM_LIMIT = 50 * 1024 * 1024


def shift(block, axis, distance):
    size = lax.axis_size(axis)
    return lax.ppermute(block, axis, [(i, (i + distance) % size) for i in range(size)])


def pick(values, index):
    return lax.dynamic_index_in_dim(values, index, 0, keepdims=False)


def gelu_pair(hidden):
    square = hidden * hidden
    tanh_val = jnp.tanh(GELU_COEF * (hidden + GELU_CUBE * square * hidden))
    activated = 0.5 * hidden * (1.0 + tanh_val)
    gradient_slope = 0.5 * (1.0 + tanh_val) + 0.5 * hidden * (
        1.0 - tanh_val * tanh_val
    ) * GELU_COEF * (1.0 + 3.0 * GELU_CUBE * square)
    return (activated, gradient_slope)


def start_weights(gathered, buffer, sems, layer, slot):
    block = gathered.shape[4]
    for zh in range(NZH):
        for y in range(NY):
            pltpu.make_async_copy(
                gathered.at[layer // SLOTS, y, layer % SLOTS, zh],
                buffer.at[slot, pl.ds((zh * NY + y) * block, block)],
                sems.at[slot],
            ).start()


def wait_weights(buffer, sems, slot):
    pltpu.make_async_copy(buffer.at[slot], buffer.at[slot], sems.at[slot]).wait()


def forward_kernel(
    meta, rows_in, gain, scale, gathered, x_old, a_old, s_old,
    rows_out, x_save, a_save, s_save,
    buffer, x_keep, a_keep, s_keep, w_sems, x_sems, a_sems, s_sems,
):
    count = meta[0]
    factor = buffer.shape[1] ** (-0.5)

    @pl.when(count > 0)
    def _():
        start_weights(gathered, buffer, w_sems, meta[1], 0)
        rows_out[...] = rows_in[...]

        def saves(layer):
            return [
                pltpu.make_async_copy(keep.at[layer], save.at[layer], sems.at[layer])
                for keep, save, sems in (
                    (x_keep, x_save, x_sems),
                    (a_keep, a_save, a_sems),
                    (s_keep, s_save, s_sems),
                )
            ]

        def step(i, carry):
            layer = meta[1 + i]
            slot = lax.rem(i, 2)

            @pl.when(i + 1 < count)
            def _():
                start_weights(gathered, buffer, w_sems, meta[2 + i], 1 - slot)

            inputs = rows_out[...]
            widened = inputs.astype(F32)
            inv_rms = lax.rsqrt(jnp.mean(widened * widened, axis=-1, keepdims=True) + NORM_EPS)
            scaled = (widened * inv_rms * gain[pl.ds(layer, 1), :]).astype(BF)
            x_keep[layer] = inputs
            a_keep[layer] = scaled
            wait_weights(buffer, w_sems, slot)
            hidden = jnp.dot(scaled, buffer[slot], preferred_element_type=F32) * factor
            activated, slope = gelu_pair(hidden)
            scale_row = scale[pl.ds(layer, 1), :]
            s_keep[layer] = slope * (scale_row * factor)
            rows_out[...] = (widened + scale_row * activated).astype(BF)
            for copy in saves(layer):
                copy.start()
            return carry

        lax.fori_loop(0, count, step, 0)

        def finish(i, carry):
            for copy in saves(meta[1 + i]):
                copy.wait()
            return carry

        lax.fori_loop(0, count, finish, 0)


def backward_kernel(
    meta, rows_in, gain, gathered, x_save, s_save, q_old,
    rows_out, q_save,
    buffer, x_keep, s_keep, q_keep, w_sems, x_sems, s_sems, q_sems,
):
    count = meta[0]

    @pl.when(count > 0)
    def _():
        start_weights(gathered, buffer, w_sems, meta[count], 0)
        rows_out[...] = rows_in[...]

        def loads(layer):
            return [
                pltpu.make_async_copy(save.at[layer], keep.at[layer], sems.at[layer])
                for keep, save, sems in ((x_keep, x_save, x_sems), (s_keep, s_save, s_sems))
            ]

        def begin(i, carry):
            for copy in loads(meta[count - i]):
                copy.start()
            return carry

        lax.fori_loop(0, count, begin, 0)

        def step(i, carry):
            layer = meta[count - i]
            slot = lax.rem(i, 2)

            @pl.when(i + 1 < count)
            def _():
                start_weights(gathered, buffer, w_sems, meta[count - i - 1], 1 - slot)

            for copy in loads(layer):
                copy.wait()
            upstream = rows_out[...].astype(F32)
            signal = (upstream * s_keep[layer]).astype(BF)
            q_keep[layer] = signal
            widened = x_keep[layer].astype(F32)
            inv_rms = lax.rsqrt(jnp.mean(widened * widened, axis=-1, keepdims=True) + NORM_EPS)
            normed = widened * inv_rms
            wait_weights(buffer, w_sems, slot)
            term = lax.dot_general(
                signal, buffer[slot], (((1,), (1,)), ((), ())), preferred_element_type=F32
            ) * gain[pl.ds(layer, 1), :]
            projection = jnp.mean(term * normed, axis=-1, keepdims=True)
            rows_out[...] = (upstream + inv_rms * (term - normed * projection)).astype(BF)
            pltpu.make_async_copy(q_keep.at[layer], q_save.at[layer], q_sems.at[layer]).start()
            return carry

        lax.fori_loop(0, count, step, 0)

        def finish(i, carry):
            layer = meta[count - i]
            pltpu.make_async_copy(q_keep.at[layer], q_save.at[layer], q_sems.at[layer]).wait()
            return carry

        lax.fori_loop(0, count, finish, 0)


def specs(names):
    kinds = {
        "s": pl.BlockSpec(memory_space=pltpu.SMEM),
        "v": pl.BlockSpec(memory_space=pltpu.VMEM),
        "a": pl.BlockSpec(memory_space=pl.ANY),
    }
    return [kinds[name] for name in names]


def forward_stage(meta, rows, gain, scale, gathered, saved):
    kept = (LAYERS,) + rows.shape
    features = rows.shape[1]
    return pl.pallas_call(
        forward_kernel,
        out_shape=[jax.ShapeDtypeStruct(rows.shape, BF)]
        + [jax.ShapeDtypeStruct(part.shape, part.dtype) for part in saved],
        in_specs=specs("svvvaaaa"),
        out_specs=specs("vaaa"),
        input_output_aliases={5: 1, 6: 2, 7: 3},
        scratch_shapes=[
            pltpu.VMEM((2, features, features), BF),
            pltpu.VMEM(kept, BF),
            pltpu.VMEM(kept, BF),
            pltpu.VMEM(kept, F32),
            pltpu.SemaphoreType.DMA((2,)),
            pltpu.SemaphoreType.DMA((LAYERS,)),
            pltpu.SemaphoreType.DMA((LAYERS,)),
            pltpu.SemaphoreType.DMA((LAYERS,)),
        ],
        compiler_params=pltpu.CompilerParams(vmem_limit_bytes=VMEM_LIMIT),
        name="stage_forward",
    )(meta, rows, gain, scale, gathered, *saved)


def backward_stage(meta, rows, gain, gathered, x_save, s_save, q_save):
    kept = (LAYERS,) + rows.shape
    features = rows.shape[1]
    return pl.pallas_call(
        backward_kernel,
        out_shape=[
            jax.ShapeDtypeStruct(rows.shape, BF),
            jax.ShapeDtypeStruct(q_save.shape, q_save.dtype),
        ],
        in_specs=specs("svvaaaa"),
        out_specs=specs("va"),
        input_output_aliases={6: 1},
        scratch_shapes=[
            pltpu.VMEM((2, features, features), BF),
            pltpu.VMEM(kept, BF),
            pltpu.VMEM(kept, F32),
            pltpu.VMEM(kept, BF),
            pltpu.SemaphoreType.DMA((2,)),
            pltpu.SemaphoreType.DMA((LAYERS,)),
            pltpu.SemaphoreType.DMA((LAYERS,)),
            pltpu.SemaphoreType.DMA((LAYERS,)),
        ],
        compiler_params=pltpu.CompilerParams(vmem_limit_bytes=VMEM_LIMIT),
        name="stage_backward",
    )(meta, rows, gain, gathered, x_save, s_save, q_save)


def gather_weights(weight_bf, core, zh):
    mine = pick(weight_bf, core)
    other = shift(pick(weight_bf, 1 - core), "core", 1)
    pair = jnp.where(
        core == 0, jnp.concatenate([mine, other]), jnp.concatenate([other, mine])
    )
    across = shift(pair, "zh", 1)
    both = jnp.where(zh == 0, jnp.stack([pair, across]), jnp.stack([across, pair]))
    full = lax.all_gather(both, ("x", "y", "core"), axis=0, tiled=False)
    return full.reshape((NX, NY, NC) + both.shape)


def to_owner(saved, x):
    pieces = [pick(saved, x)] + [
        shift(pick(saved, (x + d) % NX), "x", d) for d in range(1, NX)
    ]
    return jnp.concatenate(pieces, axis=1)


def columns_of(rows, core):
    split = rows.reshape(rows.shape[:-1] + (NZH * NY, NC, rows.shape[-1] // (NZH * NY * NC)))
    part = lax.dynamic_index_in_dim(split, core, split.ndim - 2, keepdims=False)
    return part.reshape(rows.shape[:-1] + (-1,))


def reduce_to_shard(blocks, zh, y):
    by_y = jnp.swapaxes(blocks, 0, 1)
    far = pick(by_y, (y + 2) % NY)
    from_low = shift(far[0], "y", 1)
    from_high = shift(far[1], "y", -1)
    above = pick(by_y, (y + 1) % NY)
    below = pick(by_y, (y + 3) % NY)
    above = jnp.stack([above[0] + from_low, above[1]])
    below = jnp.stack([below[0], below[1] + from_high])
    got_low = shift(above, "y", 1)
    got_high = shift(below, "y", -1)
    mine = pick(by_y, y).astype(F32) + got_low.astype(F32) + got_high.astype(F32)
    across = shift(pick(mine, 1 - zh).astype(BF), "zh", 1)
    return pick(mine, zh) + across.astype(F32)


def body(
    images,
    cotangent,
    weight,
    first_moment,
    second_moment,
    norm_gain,
    layer_scale,
    count_before,
    count_after,
    micro_order,
):
    zl, x = lax.axis_index("zl"), lax.axis_index("x")
    zh, y, core = lax.axis_index("zh"), lax.axis_index("y"), lax.axis_index("core")
    section_here = zl * NX + x
    sections = NZL * NX
    excl_before = jnp.cumsum(count_before) - count_before
    excl_after = jnp.cumsum(count_after) - count_after
    received = (excl_before - excl_after)[section_here] > 0
    last_slot = count_before[section_here] - 1
    live_count = count_after[section_here]

    plane_counts = lax.dynamic_slice_in_dim(count_before, zl * NX, NX)
    live = (jnp.arange(SLOTS)[None, :] < plane_counts[:, None]).reshape(LAYERS)
    place = jnp.where(live, jnp.cumsum(live) - 1, LAYERS)
    order = jnp.sum(
        jnp.where(place[None, :] == jnp.arange(LAYERS)[:, None], jnp.arange(LAYERS)[None, :], 0),
        axis=1,
    ).astype(jnp.int32)
    total = jnp.sum(plane_counts).astype(jnp.int32)

    def meta_for(stage):
        return jnp.concatenate([jnp.where(zl == stage, total, 0)[None], order, order[:1]])

    gathered = gather_weights(weight[0].astype(BF), core, zh)
    rows_small = lax.all_gather(
        jnp.stack([norm_gain[0], layer_scale[0]]), "x", axis=0, tiled=False
    )
    gain = rows_small[:, 0].reshape(LAYERS, -1)
    scale = rows_small[:, 1].reshape(LAYERS, -1)

    rows = pick(images, micro_order[x])
    kept = (LAYERS,) + rows.shape
    saved = [jnp.zeros(kept, BF), jnp.zeros(kept, BF), jnp.zeros(kept, F32)]
    for stage in range(NZL):
        rows, *saved = forward_stage(meta_for(stage), rows, gain, scale, gathered, saved)
        if stage + 1 < NZL:
            rows = lax.ppermute(rows, "zl", [(stage, stage + 1)])
    x_save, a_save, s_save = saved

    upstream = pick(cotangent, x)
    upstream, _ = lax.optimization_barrier((upstream, rows))
    q_save = jnp.zeros(kept, BF)
    for stage in reversed(range(NZL)):
        upstream, q_save = backward_stage(
            meta_for(stage), upstream, gain, gathered, x_save, s_save, q_save
        )
        if stage > 0:
            upstream = lax.ppermute(upstream, "zl", [(stage, stage - 1)])

    moving = [
        pick(part[0], last_slot).astype(BF) for part in (weight, first_moment, second_moment)
    ]
    moving, _ = lax.optimization_barrier((moving, x_save))
    route = [(i, i + 1) for i in range(sections - 1)]
    incoming = [lax.ppermute(part, ("zl", "x"), route).astype(F32) for part in moving]

    by_section = (NX, SLOTS) + rows.shape
    a_own = to_owner(a_save.reshape(by_section), x)
    a_mine = columns_of(a_own, core)
    a_other = shift(columns_of(a_own, 1 - core), "core", 1)
    a_all = jnp.concatenate([a_mine, a_other], axis=1)
    q_own = to_owner(q_save.reshape(by_section), x)
    q_all = jnp.concatenate([q_own, shift(q_own, "core", 1)], axis=1)

    def gradient_of(slot):
        part = lax.dot_general(
            pick(a_all, slot), pick(q_all, slot), (((0,), (0,)), ((), ())),
            preferred_element_type=F32,
        ).astype(BF)
        return reduce_to_shard(part.reshape(NZH, NY, -1, part.shape[-1]), zh, y)

    grad_last = gradient_of(last_slot)
    grad_in = lax.ppermute(grad_last.astype(BF), ("zl", "x"), route).astype(F32)
    grad_other = gradient_of(1 - last_slot)
    grad_low = jnp.where(last_slot == 0, grad_last, grad_other)
    grad_high = jnp.where(last_slot == 0, grad_other, grad_last)

    def after_move(own_low, own_high, arrived):
        return jnp.stack(
            [jnp.where(received, arrived, own_low), jnp.where(received, own_low, own_high)]
        )

    gradients = after_move(grad_low, grad_high, grad_in)
    cur_weight = after_move(weight[0, 0], weight[0, 1], incoming[0])
    cur_first = after_move(first_moment[0, 0], first_moment[0, 1], incoming[1])
    cur_second = after_move(second_moment[0, 0], second_moment[0, 1], incoming[2])
    new_first = FIRST_DECAY_RATE * cur_first + (1.0 - FIRST_DECAY_RATE) * gradients
    new_second = BETA_TWO * cur_second + (1.0 - BETA_TWO) * gradients * gradients
    updated = cur_weight - LEARN_RATE * (
        new_first / (jnp.sqrt(new_second) + ADAM_EPS) + WEIGHT_DECAY * cur_weight
    )
    live_mask = (jnp.arange(SLOTS) < live_count)[:, None, None]
    return (
        jnp.where(live_mask, updated, 0.0)[None],
        jnp.where(live_mask, new_first, 0.0)[None],
        jnp.where(live_mask, new_second, 0.0)[None],
    )


def solution(mesh):
    fine = Mesh(
        mesh.devices.reshape(NZL, NX, NZH, NY, NC), ("zl", "x", "zh", "y", "core")
    )
    section, dp = ("zl", "x"), ("zh", "y", "core")
    shards = P(section, None, dp, None)
    placed = (
        P(None, dp, None),
        P(None, dp, None),
        shards,
        shards,
        shards,
        P(section, None, None),
        P(section, None, None),
        P(),
        P(),
        P(),
    )
    return jax.shard_map(
        body, mesh=fine, in_specs=placed, out_specs=(shards, shards, shards), check_vma=False
    )
```

```python
import jax
import jax.numpy as jnp
from jax import lax
from jax.experimental import pallas as pl
from jax.experimental.pallas import tpu as pltpu
from jax.sharding import Mesh, PartitionSpec as P

NORM_EPS = 1e-06
GELU_COEF = 0.7978845608028654
GELU_CUBE = 0.044715
FIRST_DECAY_RATE = 0.9
BETA_TWO = 0.95
LEARN_RATE = 0.1
ADAM_EPS = 1e-08
WEIGHT_DECAY = 0.05

NZL, NX, NZH, NY, NC = 4, 4, 2, 4, 2
SLOTS = 2
LAYERS = NX * SLOTS
BF = jnp.bfloat16
F32 = jnp.float32
VMEM_LIMIT = 50 * 1024 * 1024
META_PLACE = 1 + LAYERS
FIRST_ROWS = 112
SOURCES = 21
FORWARD_CHUNKS = ((0, 1664),)
BACKWARD_CHUNKS = ((0, 1664),)


def shift(block, axis, distance):
    size = lax.axis_size(axis)
    return lax.ppermute(block, axis, [(i, (i + distance) % size) for i in range(size)])


def pick(values, index):
    return lax.dynamic_index_in_dim(values, index, 0, keepdims=False)


def gelu_pair(hidden):
    square = hidden * hidden
    tanh_val = jnp.tanh(GELU_COEF * (hidden + GELU_CUBE * square * hidden))
    activated = 0.5 * hidden * (1.0 + tanh_val)
    gradient_slope = 0.5 * (1.0 + tanh_val) + 0.5 * hidden * (
        1.0 - tanh_val * tanh_val
    ) * GELU_COEF * (1.0 + 3.0 * GELU_CUBE * square)
    return (activated, gradient_slope)


def start_weights(meta, sources, buffer, sems, layer, slot):
    near, pieces = sources[0], sources[1:]
    block = near.shape[3]
    section, own = layer // SLOTS, layer % SLOTS
    zh, y, x, core = [meta[META_PLACE + i] for i in range(4)]
    away = lax.rem(x - section + NX, NX)

    def copy(source, row):
        pltpu.make_async_copy(
            source,
            buffer.at[slot, pl.ds(pl.multiple_of(row, 16), source.shape[0])],
            sems.at[slot],
        ).start()

    for i in range(NY):
        copy(near.at[section, i, own], (zh * NY + i) * block)

    def rows_of(i):
        return ((1 - zh) * NY + lax.rem(y - i + NY, NY)) * block

    def copy_part(parts):
        first, second = parts[:5], parts[5:]

        for i, part in ((0, 0), (1, 1), (3, 4)):
            copy(first[part].at[away], rows_of(i))

        @pl.when(away < 2)
        def _():
            copy(first[2].at[away], rows_of(2))

        @pl.when(away >= 2)
        def _():
            copy(first[3].at[away - 2], rows_of(2))

        for i, part in ((0, 0), (1, 1), (3, 4)):

            @pl.when(away == i)
            def _(part=part):
                for j in range(NY):
                    copy(second[part].at[j], rows_of(j) + FIRST_ROWS)

        @pl.when(away == 2)
        def _():
            for j in range(NY):
                copy(second[2 + j // 2].at[j % 2], rows_of(j) + FIRST_ROWS)

    @pl.when(own == core)
    def _():
        copy_part(pieces[:10])

    @pl.when(own != core)
    def _():
        copy_part(pieces[10:])


def wait_weights(buffer, sems, slot):
    pltpu.make_async_copy(buffer.at[slot], buffer.at[slot], sems.at[slot]).wait()


def forward_kernel(*refs):
    meta, rows_in, gain, scale = refs[:4]
    sources = refs[4 : 4 + SOURCES]
    rows_out, x_save, a_save, s_save = refs[-12:-8]
    buffer, x_keep, a_keep, s_keep, w_sems, x_sems, a_sems, s_sems = refs[-8:]
    count = meta[0]
    factor = buffer.shape[1] ** (-0.5)

    @pl.when(count > 0)
    def _():
        start_weights(meta, sources, buffer, w_sems, meta[1], 0)
        rows_out[...] = rows_in[...]

        def saves(layer):
            return [
                pltpu.make_async_copy(keep.at[layer], save.at[layer], sems.at[layer])
                for keep, save, sems in (
                    (x_keep, x_save, x_sems),
                    (a_keep, a_save, a_sems),
                    (s_keep, s_save, s_sems),
                )
            ]

        def step(i, carry):
            layer = meta[1 + i]
            slot = lax.rem(i, 2)

            @pl.when(i + 1 < count)
            def _():
                start_weights(meta, sources, buffer, w_sems, meta[2 + i], 1 - slot)

            inputs = rows_out[...]
            widened = inputs.astype(F32)
            inv_rms = lax.rsqrt(jnp.mean(widened * widened, axis=-1, keepdims=True) + NORM_EPS)
            scaled = (widened * inv_rms * gain[pl.ds(layer, 1), :]).astype(BF)
            x_keep[layer] = inputs
            a_keep[layer] = scaled
            wait_weights(buffer, w_sems, slot)
            for first, width in FORWARD_CHUNKS:
                part = pl.ds(first, width)
                hidden = (
                    jnp.dot(scaled, buffer[slot, :, part], preferred_element_type=F32) * factor
                )
                activated, slope = gelu_pair(hidden)
                scale_row = scale[pl.ds(layer, 1), part]
                s_keep[layer, :, part] = slope * (scale_row * factor)
                rows_out[:, part] = (
                    x_keep[layer, :, part].astype(F32) + scale_row * activated
                ).astype(BF)
            for copy in saves(layer):
                copy.start()
            return carry

        lax.fori_loop(0, count, step, 0)

        def finish(i, carry):
            for copy in saves(meta[1 + i]):
                copy.wait()
            return carry

        lax.fori_loop(0, count, finish, 0)


def backward_kernel(*refs):
    meta, rows_in, gain, x_save, s_save = refs[:5]
    sources = refs[5 : 5 + SOURCES]
    rows_out, q_save = refs[-11:-9]
    buffer, x_keep, s_keep, q_keep, e_keep, w_sems, x_sems, s_sems, q_sems = refs[-9:]
    count = meta[0]

    @pl.when(count > 0)
    def _():
        start_weights(meta, sources, buffer, w_sems, meta[count], 0)
        rows_out[...] = rows_in[...]

        def loads(layer):
            return [
                pltpu.make_async_copy(save.at[layer], keep.at[layer], sems.at[layer])
                for keep, save, sems in ((x_keep, x_save, x_sems), (s_keep, s_save, s_sems))
            ]

        def begin(i, carry):
            for copy in loads(meta[count - i]):
                copy.start()
            return carry

        lax.fori_loop(0, count, begin, 0)

        def step(i, carry):
            layer = meta[count - i]
            slot = lax.rem(i, 2)

            @pl.when(i + 1 < count)
            def _():
                start_weights(
                    meta, sources, buffer, w_sems, meta[count - i - 1], 1 - slot
                )

            for copy in loads(layer):
                copy.wait()
            signal = (rows_out[...].astype(F32) * s_keep[layer]).astype(BF)
            q_keep[layer] = signal
            widened = x_keep[layer].astype(F32)
            inv_rms = lax.rsqrt(jnp.mean(widened * widened, axis=-1, keepdims=True) + NORM_EPS)
            wait_weights(buffer, w_sems, slot)
            total = jnp.zeros_like(inv_rms)
            for first, width in BACKWARD_CHUNKS:
                part = pl.ds(first, width)
                term = lax.dot_general(
                    signal, buffer[slot, part, :], (((1,), (1,)), ((), ())),
                    preferred_element_type=F32,
                ) * gain[pl.ds(layer, 1), part]
                e_keep[:, part] = term
                normed = x_keep[layer, :, part].astype(F32) * inv_rms
                total = total + jnp.sum(term * normed, axis=-1, keepdims=True)
            projection = total * (1.0 / e_keep.shape[1])
            rows_out[...] = (
                rows_out[...].astype(F32)
                + inv_rms * (e_keep[...] - x_keep[layer].astype(F32) * inv_rms * projection)
            ).astype(BF)
            pltpu.make_async_copy(q_keep.at[layer], q_save.at[layer], q_sems.at[layer]).start()
            return carry

        lax.fori_loop(0, count, step, 0)

        def finish(i, carry):
            layer = meta[count - i]
            pltpu.make_async_copy(q_keep.at[layer], q_save.at[layer], q_sems.at[layer]).wait()
            return carry

        lax.fori_loop(0, count, finish, 0)


def specs(names):
    kinds = {
        "s": pl.BlockSpec(memory_space=pltpu.SMEM),
        "v": pl.BlockSpec(memory_space=pltpu.VMEM),
        "a": pl.BlockSpec(memory_space=pl.ANY),
    }
    return [kinds[name] for name in names]


def forward_stage(meta, rows, gain, scale, sources, saved):
    kept = (LAYERS,) + rows.shape
    features = rows.shape[1]
    return pl.pallas_call(
        forward_kernel,
        out_shape=[jax.ShapeDtypeStruct(rows.shape, BF)]
        + [jax.ShapeDtypeStruct(kept, dtype) for dtype in (BF, BF, F32)],
        in_specs=specs("svvv" + "a" * (SOURCES + len(saved))),
        out_specs=specs("vaaa"),
        input_output_aliases={4 + SOURCES + i: 1 + i for i in range(len(saved))},
        scratch_shapes=[
            pltpu.VMEM((2, features, features), BF),
            pltpu.VMEM(kept, BF),
            pltpu.VMEM(kept, BF),
            pltpu.VMEM(kept, F32),
            pltpu.SemaphoreType.DMA((2,)),
            pltpu.SemaphoreType.DMA((LAYERS,)),
            pltpu.SemaphoreType.DMA((LAYERS,)),
            pltpu.SemaphoreType.DMA((LAYERS,)),
        ],
        compiler_params=pltpu.CompilerParams(vmem_limit_bytes=VMEM_LIMIT),
        name="stage_forward",
    )(meta, rows, gain, scale, *sources, *saved)


def backward_stage(meta, rows, gain, x_save, s_save, sources, saved):
    kept = (LAYERS,) + rows.shape
    features = rows.shape[1]
    return pl.pallas_call(
        backward_kernel,
        out_shape=[jax.ShapeDtypeStruct(rows.shape, BF), jax.ShapeDtypeStruct(kept, BF)],
        in_specs=specs("svvaa" + "a" * (SOURCES + len(saved))),
        out_specs=specs("va"),
        input_output_aliases={5 + SOURCES + i: 1 + i for i in range(len(saved))},
        scratch_shapes=[
            pltpu.VMEM((2, features, features), BF),
            pltpu.VMEM(kept, BF),
            pltpu.VMEM(kept, F32),
            pltpu.VMEM(kept, BF),
            pltpu.VMEM(rows.shape, F32),
            pltpu.SemaphoreType.DMA((2,)),
            pltpu.SemaphoreType.DMA((LAYERS,)),
            pltpu.SemaphoreType.DMA((LAYERS,)),
            pltpu.SemaphoreType.DMA((LAYERS,)),
        ],
        compiler_params=pltpu.CompilerParams(vmem_limit_bytes=VMEM_LIMIT),
        name="stage_backward",
    )(meta, rows, gain, x_save, s_save, *sources, *saved)


def around(piece, first_axis, second_axis):
    here = jnp.stack([piece] + [shift(piece, first_axis, d) for d in range(1, 4)])
    low = shift(here, second_axis, 1)
    high = shift(here, second_axis, -1)
    return [
        here,
        low,
        shift(low[:2], second_axis, 1),
        shift(high[2:], second_axis, -1),
        high,
    ]


def gather_weights(weight_bf, small, core):
    mine = pick(weight_bf, core)
    other = shift(pick(weight_bf, 1 - core), "core", 1)
    pair = jnp.where(
        core == 0, jnp.concatenate([mine, other]), jnp.concatenate([other, mine])
    )
    near = lax.all_gather(pair, ("x", "y", "core"), axis=0, tiled=False)
    small = [small] + [shift(small, "x", d) for d in range(1, NX)]
    far, small = lax.optimization_barrier((shift(pair, "zh", 1), small))
    pieces = around(far[:FIRST_ROWS], "x", "y") + around(far[FIRST_ROWS:], "y", "x")
    return (
        [near.reshape((NX, NY, NC) + pair.shape)]
        + pieces
        + [shift(piece, "core", 1) for piece in pieces]
    ), jnp.stack(small)


def to_owner(saved, roles, x):
    def piece(place):
        return jnp.stack([pick(saved, place * SLOTS + pick(slots, place)) for slots in roles])

    pieces = [piece(x)] + [shift(piece((x + d) % NX), "x", d) for d in range(1, NX)]
    return jnp.concatenate(pieces, axis=1)


def columns_of(rows, core):
    features = rows.shape[-1]
    block = features // (NZH * NY * NC)
    wanted = jnp.arange(features // NC)
    wanted = (wanted // block * NC + core) * block + wanted % block
    chosen = (wanted[:, None] == jnp.arange(features)[None, :]).astype(BF)
    return jnp.einsum("cf,srf->scr", chosen, rows, preferred_element_type=F32).astype(BF)


def reduce_to_shard(blocks, zh, y):
    by_y = jnp.swapaxes(blocks, 0, 1)
    far = pick(by_y, (y + 2) % NY)
    from_low = shift(far[0], "y", 1)
    from_high = shift(far[1], "y", -1)
    above = pick(by_y, (y + 1) % NY)
    below = pick(by_y, (y + 3) % NY)
    above = jnp.stack([above[0] + from_low, above[1]])
    below = jnp.stack([below[0], below[1] + from_high])
    got_low = shift(above, "y", 1)
    got_high = shift(below, "y", -1)
    mine = pick(by_y, y).astype(F32) + got_low.astype(F32) + got_high.astype(F32)
    across = shift(pick(mine, 1 - zh).astype(BF), "zh", 1)
    return pick(mine, zh) + across.astype(F32)


def body(
    images,
    cotangent,
    weight,
    first_moment,
    second_moment,
    norm_gain,
    layer_scale,
    count_before,
    count_after,
    micro_order,
):
    zl, x = lax.axis_index("zl"), lax.axis_index("x")
    zh, y, core = lax.axis_index("zh"), lax.axis_index("y"), lax.axis_index("core")
    section_here = zl * NX + x
    sections = NZL * NX
    excl_before = jnp.cumsum(count_before) - count_before
    excl_after = jnp.cumsum(count_after) - count_after
    received = (excl_before - excl_after)[section_here] > 0
    last_slot = count_before[section_here] - 1
    live_count = count_after[section_here]

    plane_counts = lax.dynamic_slice_in_dim(count_before, zl * NX, NX)
    live = (jnp.arange(SLOTS)[None, :] < plane_counts[:, None]).reshape(LAYERS)
    place = jnp.where(live, jnp.cumsum(live) - 1, LAYERS)
    order = jnp.sum(
        jnp.where(place[None, :] == jnp.arange(LAYERS)[:, None], jnp.arange(LAYERS)[None, :], 0),
        axis=1,
    ).astype(jnp.int32)
    total = jnp.sum(plane_counts).astype(jnp.int32)

    def meta_for(stage):
        return jnp.concatenate(
            [jnp.where(zl == stage, total, 0)[None], order, jnp.stack([zh, y, x, core])]
        )

    small = jnp.stack([norm_gain[0], layer_scale[0]])
    sources, small = gather_weights(weight[0].astype(BF), small, core)
    small = jnp.stack([pick(small, (x - i) % NX) for i in range(NX)])
    gain = small[:, 0].reshape(LAYERS, -1)
    scale = small[:, 1].reshape(LAYERS, -1)

    rows = pick(images, micro_order[x])
    saved = []
    for stage in range(NZL):
        rows, *saved = forward_stage(meta_for(stage), rows, gain, scale, sources, saved)
        if stage + 1 < NZL:
            rows = lax.ppermute(rows, "zl", [(stage, stage + 1)])
    x_save, a_save, s_save = saved

    last_slots = plane_counts - 1
    a_own = to_owner(a_save, (last_slots, 1 - last_slots), x)
    a_mine = columns_of(a_own, core)
    a_other = shift(columns_of(a_own, 1 - core), "core", 1)

    upstream = pick(cotangent, x)
    saved = []
    for stage in reversed(range(NZL)):
        if stage == 0:
            upstream, a_mine, a_other = lax.optimization_barrier((upstream, a_mine, a_other))
        upstream, *saved = backward_stage(
            meta_for(stage), upstream, gain, x_save, s_save, sources, saved
        )
        if stage > 0:
            upstream = lax.ppermute(upstream, "zl", [(stage, stage - 1)])
    q_save = saved[0]

    def gradient_of(q_own, role):
        part = (
            jnp.dot(a_mine[role], q_own, preferred_element_type=F32)
            + jnp.dot(a_other[role], shift(q_own, "core", 1), preferred_element_type=F32)
        ).astype(BF)
        return reduce_to_shard(part.reshape(NZH, NY, -1, part.shape[-1]), zh, y)

    q_last = to_owner(q_save, (last_slots,), x)[0]
    q_save, _ = lax.optimization_barrier((q_save, q_last))
    q_other = to_owner(q_save, (1 - last_slots,), x)[0]

    moving = jnp.stack(
        [pick(part[0], last_slot).astype(BF) for part in (weight, first_moment, second_moment)]
    )
    moving, _ = lax.optimization_barrier((moving, q_other))
    route = [(i, i + 1) for i in range(sections - 1)]
    incoming = lax.ppermute(moving, ("zl", "x"), route).astype(F32)

    grad_last = gradient_of(q_last, 0)
    grad_in = lax.ppermute(grad_last.astype(BF), ("zl", "x"), route).astype(F32)
    grad_other = gradient_of(q_other, 1)
    grad_low = jnp.where(last_slot == 0, grad_last, grad_other)
    grad_high = jnp.where(last_slot == 0, grad_other, grad_last)

    def after_move(own_low, own_high, arrived):
        return jnp.stack(
            [jnp.where(received, arrived, own_low), jnp.where(received, own_low, own_high)]
        )

    gradients = after_move(grad_low, grad_high, grad_in)
    cur_weight = after_move(weight[0, 0], weight[0, 1], incoming[0])
    cur_first = after_move(first_moment[0, 0], first_moment[0, 1], incoming[1])
    cur_second = after_move(second_moment[0, 0], second_moment[0, 1], incoming[2])
    new_first = FIRST_DECAY_RATE * cur_first + (1.0 - FIRST_DECAY_RATE) * gradients
    new_second = BETA_TWO * cur_second + (1.0 - BETA_TWO) * gradients * gradients
    updated = cur_weight - LEARN_RATE * (
        new_first / (jnp.sqrt(new_second) + ADAM_EPS) + WEIGHT_DECAY * cur_weight
    )
    live_mask = (jnp.arange(SLOTS) < live_count)[:, None, None]
    return (
        jnp.where(live_mask, updated, 0.0)[None],
        jnp.where(live_mask, new_first, 0.0)[None],
        jnp.where(live_mask, new_second, 0.0)[None],
    )


def solution(mesh):
    fine = Mesh(
        mesh.devices.reshape(NZL, NX, NZH, NY, NC), ("zl", "x", "zh", "y", "core")
    )
    section, dp = ("zl", "x"), ("zh", "y", "core")
    shards = P(section, None, dp, None)
    placed = (
        P(None, dp, None),
        P(None, dp, None),
        shards,
        shards,
        shards,
        P(section, None, None),
        P(section, None, None),
        P(),
        P(),
        P(),
    )
    return jax.shard_map(
        body, mesh=fine, in_specs=placed, out_specs=(shards, shards, shards), check_vma=False
    )
```

```python
import jax
import jax.numpy as jnp
from jax import lax
from jax.experimental import pallas as pl
from jax.experimental.pallas import tpu as pltpu
from jax.sharding import Mesh, PartitionSpec as P

NORM_EPS = 1e-06
GELU_COEF = 0.7978845608028654
GELU_CUBE = 0.044715
FIRST_DECAY_RATE = 0.9
BETA_TWO = 0.95
LEARN_RATE = 0.1
ADAM_EPS = 1e-08
WEIGHT_DECAY = 0.05

NZL, NX, NZH, NY, NC = 4, 4, 2, 4, 2
SLOTS = 2
LAYERS = NX * SLOTS
BF = jnp.bfloat16
F32 = jnp.float32
VMEM_LIMIT = 50 * 1024 * 1024
META_PLACE = 1 + LAYERS
FIRST_ROWS = 112
SOURCES = 21
FORWARD_CHUNKS = ((0, 1664),)
BACKWARD_CHUNKS = ((0, 1664),)


def shift(block, axis, distance):
    size = lax.axis_size(axis)
    return lax.ppermute(block, axis, [(i, (i + distance) % size) for i in range(size)])


def pick(values, index):
    return lax.dynamic_index_in_dim(values, index, 0, keepdims=False)


def gelu_pair(hidden):
    square = hidden * hidden
    tanh_val = jnp.tanh(GELU_COEF * (hidden + GELU_CUBE * square * hidden))
    activated = 0.5 * hidden * (1.0 + tanh_val)
    gradient_slope = 0.5 * (1.0 + tanh_val) + 0.5 * hidden * (
        1.0 - tanh_val * tanh_val
    ) * GELU_COEF * (1.0 + 3.0 * GELU_CUBE * square)
    return (activated, gradient_slope)


def start_weights(meta, sources, buffer, sems, layer, slot):
    near, pieces = sources[0], sources[1:]
    block = near.shape[3]
    section, own = layer // SLOTS, layer % SLOTS
    zh, y, x, core = [meta[META_PLACE + i] for i in range(4)]
    away = lax.rem(x - section + NX, NX)

    def copy(source, row):
        pltpu.make_async_copy(
            source,
            buffer.at[slot, pl.ds(pl.multiple_of(row, 16), source.shape[0])],
            sems.at[slot],
        ).start()

    for i in range(NY):
        copy(near.at[section, i, own], (zh * NY + i) * block)

    def rows_of(i):
        return ((1 - zh) * NY + lax.rem(y - i + NY, NY)) * block

    def copy_part(parts):
        first, second = parts[:5], parts[5:]

        for i, part in ((0, 0), (1, 1), (3, 4)):
            copy(first[part].at[away], rows_of(i))

        @pl.when(away < 2)
        def _():
            copy(first[2].at[away], rows_of(2))

        @pl.when(away >= 2)
        def _():
            copy(first[3].at[away - 2], rows_of(2))

        for i, part in ((0, 0), (1, 1), (3, 4)):

            @pl.when(away == i)
            def _(part=part):
                for j in range(NY):
                    copy(second[part].at[j], rows_of(j) + FIRST_ROWS)

        @pl.when(away == 2)
        def _():
            for j in range(NY):
                copy(second[2 + j // 2].at[j % 2], rows_of(j) + FIRST_ROWS)

    @pl.when(own == core)
    def _():
        copy_part(pieces[:10])

    @pl.when(own != core)
    def _():
        copy_part(pieces[10:])


def wait_weights(buffer, sems, slot):
    pltpu.make_async_copy(buffer.at[slot], buffer.at[slot], sems.at[slot]).wait()


def forward_kernel(*refs):
    meta, rows_in, gain, scale = refs[:4]
    sources = refs[4 : 4 + SOURCES]
    rows_out, x_save, a_save, s_save = refs[-12:-8]
    buffer, x_keep, a_keep, s_keep, w_sems, x_sems, a_sems, s_sems = refs[-8:]
    count = meta[0]
    factor = buffer.shape[1] ** (-0.5)

    @pl.when(count > 0)
    def _():
        start_weights(meta, sources, buffer, w_sems, meta[1], 0)
        rows_out[...] = rows_in[...]

        def saves(layer):
            return [
                pltpu.make_async_copy(keep.at[layer], save.at[layer], sems.at[layer])
                for keep, save, sems in (
                    (x_keep, x_save, x_sems),
                    (a_keep, a_save, a_sems),
                    (s_keep, s_save, s_sems),
                )
            ]

        def step(i, carry):
            layer = meta[1 + i]
            slot = lax.rem(i, 2)

            @pl.when(i + 1 < count)
            def _():
                start_weights(meta, sources, buffer, w_sems, meta[2 + i], 1 - slot)

            inputs = rows_out[...]
            widened = inputs.astype(F32)
            inv_rms = lax.rsqrt(jnp.mean(widened * widened, axis=-1, keepdims=True) + NORM_EPS)
            scaled = (widened * inv_rms * gain[pl.ds(layer, 1), :]).astype(BF)
            x_keep[layer] = inputs
            a_keep[layer] = scaled
            wait_weights(buffer, w_sems, slot)
            for first, width in FORWARD_CHUNKS:
                part = pl.ds(first, width)
                hidden = (
                    jnp.dot(scaled, buffer[slot, :, part], preferred_element_type=F32) * factor
                )
                activated, slope = gelu_pair(hidden)
                scale_row = scale[pl.ds(layer, 1), part]
                s_keep[layer, :, part] = slope * (scale_row * factor)
                rows_out[:, part] = (
                    x_keep[layer, :, part].astype(F32) + scale_row * activated
                ).astype(BF)
            for copy in saves(layer):
                copy.start()
            return carry

        lax.fori_loop(0, count, step, 0)

        def finish(i, carry):
            for copy in saves(meta[1 + i]):
                copy.wait()
            return carry

        lax.fori_loop(0, count, finish, 0)


def backward_kernel(*refs):
    meta, rows_in, gain, x_save, s_save = refs[:5]
    sources = refs[5 : 5 + SOURCES]
    rows_out, q_save = refs[-11:-9]
    buffer, x_keep, s_keep, q_keep, e_keep, w_sems, x_sems, s_sems, q_sems = refs[-9:]
    count = meta[0]

    @pl.when(count > 0)
    def _():
        start_weights(meta, sources, buffer, w_sems, meta[count], 0)
        rows_out[...] = rows_in[...]

        def loads(layer):
            return [
                pltpu.make_async_copy(save.at[layer], keep.at[layer], sems.at[layer])
                for keep, save, sems in ((x_keep, x_save, x_sems), (s_keep, s_save, s_sems))
            ]

        def begin(i, carry):
            for copy in loads(meta[count - i]):
                copy.start()
            return carry

        lax.fori_loop(0, count, begin, 0)

        def step(i, carry):
            layer = meta[count - i]
            slot = lax.rem(i, 2)

            @pl.when(i + 1 < count)
            def _():
                start_weights(
                    meta, sources, buffer, w_sems, meta[count - i - 1], 1 - slot
                )

            for copy in loads(layer):
                copy.wait()
            signal = (rows_out[...].astype(F32) * s_keep[layer]).astype(BF)
            q_keep[layer] = signal
            widened = x_keep[layer].astype(F32)
            inv_rms = lax.rsqrt(jnp.mean(widened * widened, axis=-1, keepdims=True) + NORM_EPS)
            wait_weights(buffer, w_sems, slot)
            total = jnp.zeros_like(inv_rms)
            for first, width in BACKWARD_CHUNKS:
                part = pl.ds(first, width)
                term = lax.dot_general(
                    signal, buffer[slot, part, :], (((1,), (1,)), ((), ())),
                    preferred_element_type=F32,
                ) * gain[pl.ds(layer, 1), part]
                e_keep[:, part] = term
                normed = x_keep[layer, :, part].astype(F32) * inv_rms
                total = total + jnp.sum(term * normed, axis=-1, keepdims=True)
            projection = total * (1.0 / e_keep.shape[1])
            rows_out[...] = (
                rows_out[...].astype(F32)
                + inv_rms * (e_keep[...] - x_keep[layer].astype(F32) * inv_rms * projection)
            ).astype(BF)
            pltpu.make_async_copy(q_keep.at[layer], q_save.at[layer], q_sems.at[layer]).start()
            return carry

        lax.fori_loop(0, count, step, 0)

        def finish(i, carry):
            layer = meta[count - i]
            pltpu.make_async_copy(q_keep.at[layer], q_save.at[layer], q_sems.at[layer]).wait()
            return carry

        lax.fori_loop(0, count, finish, 0)


def specs(names):
    kinds = {
        "s": pl.BlockSpec(memory_space=pltpu.SMEM),
        "v": pl.BlockSpec(memory_space=pltpu.VMEM),
        "a": pl.BlockSpec(memory_space=pl.ANY),
    }
    return [kinds[name] for name in names]


def forward_stage(meta, rows, gain, scale, sources, saved):
    kept = (LAYERS,) + rows.shape
    features = rows.shape[1]
    return pl.pallas_call(
        forward_kernel,
        out_shape=[jax.ShapeDtypeStruct(rows.shape, BF)]
        + [jax.ShapeDtypeStruct(kept, dtype) for dtype in (BF, BF, F32)],
        in_specs=specs("svvv" + "a" * (SOURCES + len(saved))),
        out_specs=specs("vaaa"),
        input_output_aliases={4 + SOURCES + i: 1 + i for i in range(len(saved))},
        scratch_shapes=[
            pltpu.VMEM((2, features, features), BF),
            pltpu.VMEM(kept, BF),
            pltpu.VMEM(kept, BF),
            pltpu.VMEM(kept, F32),
            pltpu.SemaphoreType.DMA((2,)),
            pltpu.SemaphoreType.DMA((LAYERS,)),
            pltpu.SemaphoreType.DMA((LAYERS,)),
            pltpu.SemaphoreType.DMA((LAYERS,)),
        ],
        compiler_params=pltpu.CompilerParams(vmem_limit_bytes=VMEM_LIMIT),
        name="stage_forward",
    )(meta, rows, gain, scale, *sources, *saved)


def backward_stage(meta, rows, gain, x_save, s_save, sources, saved):
    kept = (LAYERS,) + rows.shape
    features = rows.shape[1]
    return pl.pallas_call(
        backward_kernel,
        out_shape=[jax.ShapeDtypeStruct(rows.shape, BF), jax.ShapeDtypeStruct(kept, BF)],
        in_specs=specs("svvaa" + "a" * (SOURCES + len(saved))),
        out_specs=specs("va"),
        input_output_aliases={5 + SOURCES + i: 1 + i for i in range(len(saved))},
        scratch_shapes=[
            pltpu.VMEM((2, features, features), BF),
            pltpu.VMEM(kept, BF),
            pltpu.VMEM(kept, F32),
            pltpu.VMEM(kept, BF),
            pltpu.VMEM(rows.shape, F32),
            pltpu.SemaphoreType.DMA((2,)),
            pltpu.SemaphoreType.DMA((LAYERS,)),
            pltpu.SemaphoreType.DMA((LAYERS,)),
            pltpu.SemaphoreType.DMA((LAYERS,)),
        ],
        compiler_params=pltpu.CompilerParams(vmem_limit_bytes=VMEM_LIMIT),
        name="stage_backward",
    )(meta, rows, gain, x_save, s_save, *sources, *saved)


def around(piece, first_axis, second_axis):
    here = jnp.stack([piece] + [shift(piece, first_axis, d) for d in range(1, 4)])
    low = shift(here, second_axis, 1)
    high = shift(here, second_axis, -1)
    return [
        here,
        low,
        shift(low[:2], second_axis, 1),
        shift(high[2:], second_axis, -1),
        high,
    ]


def gather_weights(weight_bf, small, core):
    mine = pick(weight_bf, core)
    other = shift(pick(weight_bf, 1 - core), "core", 1)
    pair = jnp.where(
        core == 0, jnp.concatenate([mine, other]), jnp.concatenate([other, mine])
    )
    near = lax.all_gather(pair, ("x", "y", "core"), axis=0, tiled=False)
    small = [small] + [shift(small, "x", d) for d in range(1, NX)]
    far, small = lax.optimization_barrier((shift(pair, "zh", 1), small))
    pieces = around(far[:FIRST_ROWS], "x", "y") + around(far[FIRST_ROWS:], "y", "x")
    return (
        [near.reshape((NX, NY, NC) + pair.shape)]
        + pieces
        + [shift(piece, "core", 1) for piece in pieces]
    ), jnp.stack(small)


def to_owner(saved, roles, x):
    def piece(place):
        return jnp.stack([pick(saved, place * SLOTS + pick(slots, place)) for slots in roles])

    pieces = [piece(x)] + [shift(piece((x + d) % NX), "x", d) for d in range(1, NX)]
    return jnp.concatenate(pieces, axis=1)


def columns_of(rows, core):
    features = rows.shape[-1]
    block = features // (NZH * NY * NC)
    wanted = jnp.arange(features // NC)
    wanted = (wanted // block * NC + core) * block + wanted % block
    chosen = (wanted[:, None] == jnp.arange(features)[None, :]).astype(BF)
    return jnp.einsum("cf,srf->scr", chosen, rows, preferred_element_type=F32).astype(BF)


def reduce_to_shard(blocks, zh, y):
    by_y = jnp.swapaxes(blocks, 0, 1)
    far = pick(by_y, (y + 2) % NY)
    from_low = shift(far[0], "y", 1)
    from_high = shift(far[1], "y", -1)
    above = pick(by_y, (y + 1) % NY)
    below = pick(by_y, (y + 3) % NY)
    above = jnp.stack([above[0] + from_low, above[1]])
    below = jnp.stack([below[0], below[1] + from_high])
    got_low = shift(above, "y", 1)
    got_high = shift(below, "y", -1)
    mine = pick(by_y, y).astype(F32) + got_low.astype(F32) + got_high.astype(F32)
    across = shift(pick(mine, 1 - zh).astype(BF), "zh", 1)
    return pick(mine, zh) + across.astype(F32)


def body(
    images,
    cotangent,
    weight,
    first_moment,
    second_moment,
    norm_gain,
    layer_scale,
    count_before,
    count_after,
    micro_order,
):
    zl, x = lax.axis_index("zl"), lax.axis_index("x")
    zh, y, core = lax.axis_index("zh"), lax.axis_index("y"), lax.axis_index("core")
    section_here = zl * NX + x
    sections = NZL * NX
    excl_before = jnp.cumsum(count_before) - count_before
    excl_after = jnp.cumsum(count_after) - count_after
    received = (excl_before - excl_after)[section_here] > 0
    last_slot = count_before[section_here] - 1
    live_count = count_after[section_here]

    plane_counts = lax.dynamic_slice_in_dim(count_before, zl * NX, NX)
    live = (jnp.arange(SLOTS)[None, :] < plane_counts[:, None]).reshape(LAYERS)
    place = jnp.where(live, jnp.cumsum(live) - 1, LAYERS)
    order = jnp.sum(
        jnp.where(place[None, :] == jnp.arange(LAYERS)[:, None], jnp.arange(LAYERS)[None, :], 0),
        axis=1,
    ).astype(jnp.int32)
    total = jnp.sum(plane_counts).astype(jnp.int32)

    def meta_for(stage):
        return jnp.concatenate(
            [jnp.where(zl == stage, total, 0)[None], order, jnp.stack([zh, y, x, core])]
        )

    small = jnp.stack([norm_gain[0], layer_scale[0]])
    sources, small = gather_weights(weight[0].astype(BF), small, core)
    small = jnp.stack([pick(small, (x - i) % NX) for i in range(NX)])
    gain = small[:, 0].reshape(LAYERS, -1)
    scale = small[:, 1].reshape(LAYERS, -1)

    rows = pick(images, micro_order[x])
    saved = []
    for stage in range(NZL):
        rows, *saved = forward_stage(meta_for(stage), rows, gain, scale, sources, saved)
        if stage + 1 < NZL:
            rows = lax.ppermute(rows, "zl", [(stage, stage + 1)])
    x_save, a_save, s_save = saved

    last_slots = plane_counts - 1
    a_own = to_owner(a_save, (last_slots, 1 - last_slots), x)
    a_mine = columns_of(a_own, core)
    a_other = shift(columns_of(a_own, 1 - core), "core", 1)

    upstream = pick(cotangent, x)
    saved = []
    for stage in reversed(range(NZL)):
        if stage == 0:
            upstream, a_mine, a_other = lax.optimization_barrier((upstream, a_mine, a_other))
        upstream, *saved = backward_stage(
            meta_for(stage), upstream, gain, x_save, s_save, sources, saved
        )
        if stage > 0:
            upstream = lax.ppermute(upstream, "zl", [(stage, stage - 1)])
    q_save = saved[0]

    def partial_of(q_own, role):
        part = (
            jnp.dot(a_mine[role], q_own, preferred_element_type=F32)
            + jnp.dot(a_other[role], shift(q_own, "core", 1), preferred_element_type=F32)
        ).astype(BF)
        return part.reshape(NZH, NY, -1, part.shape[-1])

    part_last = partial_of(to_owner(q_save, (last_slots,), x)[0], 0)
    part_last, q_save = lax.optimization_barrier((part_last, q_save))
    grad_last = reduce_to_shard(part_last, zh, y)
    q_other = to_owner(q_save, (1 - last_slots,), x)[0]

    moving = jnp.stack(
        [pick(part[0], last_slot).astype(BF) for part in (weight, first_moment, second_moment)]
    )
    moving, _ = lax.optimization_barrier((moving, q_other))
    route = [(i, i + 1) for i in range(sections - 1)]
    incoming = lax.ppermute(moving, ("zl", "x"), route)

    grad_in = lax.ppermute(grad_last.astype(BF), ("zl", "x"), route).astype(F32)
    grad_other = reduce_to_shard(partial_of(q_other, 1), zh, y)
    incoming, grad_other = lax.optimization_barrier((incoming, grad_other))
    incoming = incoming.astype(F32)
    grad_low = jnp.where(last_slot == 0, grad_last, grad_other)
    grad_high = jnp.where(last_slot == 0, grad_other, grad_last)

    def after_move(own_low, own_high, arrived):
        return jnp.stack(
            [jnp.where(received, arrived, own_low), jnp.where(received, own_low, own_high)]
        )

    gradients = after_move(grad_low, grad_high, grad_in)
    cur_weight = after_move(weight[0, 0], weight[0, 1], incoming[0])
    cur_first = after_move(first_moment[0, 0], first_moment[0, 1], incoming[1])
    cur_second = after_move(second_moment[0, 0], second_moment[0, 1], incoming[2])
    new_first = FIRST_DECAY_RATE * cur_first + (1.0 - FIRST_DECAY_RATE) * gradients
    new_second = BETA_TWO * cur_second + (1.0 - BETA_TWO) * gradients * gradients
    updated = cur_weight - LEARN_RATE * (
        new_first / (jnp.sqrt(new_second) + ADAM_EPS) + WEIGHT_DECAY * cur_weight
    )
    live_mask = (jnp.arange(SLOTS) < live_count)[:, None, None]
    return (
        jnp.where(live_mask, updated, 0.0)[None],
        jnp.where(live_mask, new_first, 0.0)[None],
        jnp.where(live_mask, new_second, 0.0)[None],
    )


def solution(mesh):
    fine = Mesh(
        mesh.devices.reshape(NZL, NX, NZH, NY, NC), ("zl", "x", "zh", "y", "core")
    )
    section, dp = ("zl", "x"), ("zh", "y", "core")
    shards = P(section, None, dp, None)
    placed = (
        P(None, dp, None),
        P(None, dp, None),
        shards,
        shards,
        shards,
        P(section, None, None),
        P(section, None, None),
        P(),
        P(),
        P(),
    )
    return jax.shard_map(
        body, mesh=fine, in_specs=placed, out_specs=(shards, shards, shards), check_vma=False
    )
```
